512 devices in a mesh: row: 64 (over z_lo, y, core), rep: 8 (over x, z_hi).
Axes of the slice: x: 4, y: 8, z: 8 (z_hi: 2, z_lo: 4; z = z_hi * 4 + z_lo), core: 2. Of those that a mesh axis runs over, the one named last changes fastest.
Arguments:
- features: float32 [131072, 256], P(('row', 'rep')), may hold values from -6 to 6
- weight: float32 [256, 256], replicated, may hold values from -0.375 to 0.375
- cotangent: float32 [131072, 256], P(('row', 'rep')), may hold values from -6 to 6
- tile_values: float32 [64, 8, 40, 128, 128], P('row', 'rep'), may hold values from -0.125 to 0.125
- tile_pos: int32 [64, 8, 40], P('row', 'rep'), may hold values from 0 to 127, as said below
- tile_count: int32 [64, 8], P('row', 'rep'), may hold values from 5 to 40, as said below
Outputs:
- activation: float32 [131072, 256], P(('row', 'rep'))
- grad_features: float32 [131072, 256], P(('row', 'rep'))
- grad_weight: float32 [256, 256], replicated
The draws below stay inside these ranges and needn't reach their ends.
Inputs may be any that keep to these rules, and one draw needn't show every extreme that they name: `tile_pos`: the 40 slots of one device hold distinct positions. `tile_count`: some device has all 40 slots live.
All inputs are finite; a program needn't handle non-finite values.
Results may differ from the reference program's by a relative error of at most 0.0003.
Values sent between devices are 32-bit elements; how exact they have to be, the bound alone decides.
A program may use at most 64 MiB of HBM per device.

```python
import math
import jax
import jax.numpy as jnp
from jax import lax

HID = 256
TILE = 128
STOPS = 4
KMAX = 40
ROWS_DEV = 2048
SLABS = 64
GROUPS = 8
TILE_ROWS = 16
SHARE_TILES = 2
NODES = 131072
N_REP = 8


def draw_tile_pos(key, part):
    key = jax.random.fold_in(key, 11)
    positions = ROWS_DEV // TILE * STOPS * (ROWS_DEV // (TILE * GROUPS))
    keys = jax.random.split(key, SLABS * GROUPS)

    def pick_slots(one_key):
        return jax.random.permutation(one_key, positions)[:KMAX]
    chosen = jax.vmap(pick_slots)(keys)
    return chosen.reshape(SLABS, GROUPS, KMAX).astype(jnp.int32)


def draw_tile_count(key, part):
    key = jax.random.fold_in(key, 23)
    first_key, second_key = jax.random.split(key)
    halvings = jax.random.randint(first_key, (SLABS * GROUPS,), 0, 4)
    counts = KMAX // jnp.left_shift(jnp.ones_like(halvings), halvings)
    busiest = jax.random.randint(second_key, (), 0, SLABS * GROUPS)
    counts = counts.at[busiest].set(KMAX)
    return counts.reshape(SLABS, GROUPS).astype(jnp.int32)


def levels(key, dims, cuts, low, high):
    def one(position, parts):
        heights = jax.random.uniform(jax.random.fold_in(jax.random.fold_in(key, 6), position), (parts,), jnp.float32, low / len(cuts), high / len(cuts))
        return jnp.repeat(jnp.exp(heights), dims[position] // parts).reshape((-1,) + (1,) * (len(dims) - position - 1))

    level = one(*cuts[0])
    for cut in cuts[1:]:
        level = level * one(*cut)
    return level


def centred(key, dims, scale, most, shards=(), dtype=jnp.bfloat16):
    result = jax.random.normal(key, dims, jnp.float32) * scale
    if len(shards) > 0:
        result = levels(key, dims, shards, -0.22, 0.18) * result
    return jnp.clip(result, min=-most, max=most).astype(dtype)


def setup_inputs(seed: int = 0) -> dict:
    key_list = jax.random.split(jax.random.key(seed), 7)
    features = centred(key_list[0], (NODES, HID), 1.0, 6.0, ((0, 512),), jnp.float32)
    weight = centred(key_list[1], (HID, HID), HID ** -0.5, 0.375, (), jnp.float32)
    cotangent = centred(key_list[2], (NODES, HID), 1.0, 6.0, ((0, 512),), jnp.float32)
    tile_values = centred(key_list[3], (SLABS, GROUPS, KMAX, TILE, TILE), (TILE * KMAX * N_REP // (ROWS_DEV // TILE)) ** -0.5, 0.125, ((0, 64), (1, 8)), jnp.float32)
    tile_pos = draw_tile_pos(jax.random.fold_in(key_list[6], 71), 0)
    tile_count = draw_tile_count(jax.random.fold_in(key_list[6], 71), 0)
    return {"features": features, "weight": weight, "cotangent": cotangent, "tile_values": tile_values, "tile_pos": tile_pos, "tile_count": tile_count}


def aggregate_blocks(band, tile_values, tile_pos, tile_count, tile_rows):
    columns = band.shape[0]
    source = tile_pos % columns
    target = tile_pos // columns
    picked = jnp.take(band, source, axis=0)
    product = jnp.einsum('kij,kjh->kih', tile_values, picked, precision=lax.Precision.HIGHEST)
    live_slots = (jnp.arange(tile_values.shape[0]) < tile_count).astype(jnp.float32)
    onehot = (target[None, :] == jnp.arange(tile_rows)[:, None]).astype(jnp.float32) * live_slots[None, :]
    summed = jnp.einsum('tk,kih->tih', onehot, product, precision=lax.Precision.HIGHEST)
    return summed.reshape(tile_rows * band.shape[1], band.shape[2])

def spread_back(rows_grad, tile_values, tile_pos, tile_count, positions):
    source = tile_pos % positions
    target = tile_pos // positions
    picked = jnp.take(rows_grad, target, axis=0)
    contrib = jnp.einsum('kji,kjh->kih', tile_values, picked, precision=lax.Precision.HIGHEST)
    live_slots = (jnp.arange(tile_values.shape[0]) < tile_count).astype(jnp.float32)
    onehot = (source[None, :] == jnp.arange(positions)[:, None]).astype(jnp.float32) * live_slots[None, :]
    return jnp.einsum('qk,kih->qih', onehot, contrib, precision=lax.Precision.HIGHEST)

def reference(features, weight, cotangent, tile_values, tile_pos, tile_count):
    shares = features.reshape(SLABS, GROUPS, SHARE_TILES, TILE, HID)
    band = jnp.stack([jnp.roll(shares, stop, axis=0) for stop in range(STOPS)], axis=2)
    band = band.reshape(SLABS, GROUPS, STOPS * SHARE_TILES, TILE, HID)

    def slab_aggregate(items):
        band_slab, values_slab, pos_slab, count_slab = items

        def one_device(band_here, values_here, pos_here, count_here):
            return aggregate_blocks(band_here, values_here, pos_here, count_here, TILE_ROWS)
        partial_value = jax.vmap(one_device)(band_slab, values_slab, pos_slab, count_slab)
        return lax.optimization_barrier(jnp.sum(partial_value, axis=0))
    aggregate = lax.map(slab_aggregate, (band, tile_values, tile_pos, tile_count)).reshape(NODES, HID)
    preact = jnp.dot(aggregate, weight, precision=lax.Precision.HIGHEST, preferred_element_type=jnp.float32)
    squashed = jax.nn.sigmoid(preact)
    activation = preact * squashed
    slopes = cotangent * squashed * (1.0 + preact * (1.0 - squashed))
    back_grad = jnp.dot(slopes, weight.T, precision=lax.Precision.HIGHEST, preferred_element_type=jnp.float32)
    grad_weight = jnp.dot(aggregate.T, slopes, precision=lax.Precision.HIGHEST, preferred_element_type=jnp.float32) / math.sqrt(NODES)
    rows_grad = back_grad.reshape(SLABS, TILE_ROWS, TILE, HID)

    def slab_spread(items):
        rows_slab, values_slab, pos_slab, count_slab = items

        def one_device(values_here, pos_here, count_here):
            return spread_back(rows_slab, values_here, pos_here, count_here, STOPS * SHARE_TILES)
        return jax.vmap(one_device)(values_slab, pos_slab, count_slab)
    spread = lax.map(slab_spread, (rows_grad, tile_values, tile_pos, tile_count))
    spread = spread.reshape(SLABS, GROUPS, STOPS, SHARE_TILES * TILE, HID)
    grad_features = spread[:, :, 0]
    for stop in range(1, STOPS):
        grad_features = grad_features + jnp.roll(spread[:, :, stop], -stop, axis=0)
    return (activation, grad_features.reshape(NODES, HID), grad_weight)
```

```python
import functools
import math

import jax
import jax.numpy as jnp
from jax import lax
from jax.experimental import pallas as pl
from jax.experimental.pallas import tpu as pltpu
from jax.sharding import PartitionSpec as P

HID = 256
TILE = 128
STOPS = 4
KMAX = 40
ROWS = 256
HALF = 128
NX = 4
NY = 8
NZ = 8
SLABS = 64
MESH = pl.DeviceIdType.MESH
BF = jnp.bfloat16
F32 = jnp.float32


def split(value):
    high = value.astype(BF)
    low = (value - high.astype(F32)).astype(BF)
    return high, low


def dot(a, b, contract=((1,), (0,))):
    return lax.dot_general(a, b, (contract, ((), ())), preferred_element_type=F32)


def dot3(a, b, contract=((1,), (0,))):
    a_hi, a_lo = a
    b_hi, b_lo = b
    return dot(a_hi, b_hi, contract) + (dot(a_hi, b_lo, contract) + dot(a_lo, b_hi, contract))


def kernel(
    inv, feat, weight, cot, tiles_hbm, act, gf, gw,
    tiles, a_hi, a_lo, t_hi, t_lo, band, x_cat, pbuf, rx1, rx2, zsend, zrecv, mine,
    g, sp, rr, lw, cr, yr, xr, zz, wh, gwb,
    load_sem, band_s, band_r, rs_s, rs_r, zx_s, zx_r, ag_s, ag_r, az_s, az_r, ring_s, ring_r,
    red_s, red_r,
):
    row = lax.axis_index("row")
    rep = lax.axis_index("rep")
    core = lax.rem(row, 2)
    y = lax.rem(row // 2, NY)
    z_lo = row // 16
    x = rep // 2
    z_hi = lax.rem(rep, 2)
    z = z_hi * 4 + z_lo

    def device(core_, y_, z_, x_):
        return (lax.rem(z_, 4) * 16 + y_ * 2 + core_, x_ * 2 + z_ // 4)

    x_right = lax.rem(x + 1, NX)
    x_opp = lax.rem(x + 2, NX)
    x_left = lax.rem(x + 3, NX)
    right = (row, x_right * 2 + z_hi)
    left = (row, x_left * 2 + z_hi)
    across = (row, x * 2 + 1 - z_hi)
    partner = (row + 1 - 2 * core, rep)
    following = (lax.rem(row + 1, SLABS), rep)
    previous = (lax.rem(row + SLABS - 1, SLABS), rep)
    y_peers = [device(core, lax.rem(y + k, NY), z, x) for k in range(1, NY)]
    x_peers = [device(core, y, z, lax.rem(x + k, NX)) for k in range(1, NX)]
    z_peers = [device(core, y, lax.rem(z + k, NZ), x) for k in range(1, NZ)]

    started = []

    def send(src, dst, s_sem, r_sem, to):
        copy = pltpu.make_async_remote_copy(
            src_ref=src, dst_ref=dst, send_sem=s_sem, recv_sem=r_sem,
            device_id=to, device_id_type=MESH,
        )
        copy.start()
        started.append(copy)
        return copy

    loads = [
        pltpu.make_async_copy(feat.at[:, pl.ds(c * HALF, HALF)], band.at[0, c], load_sem.at[c])
        for c in range(2)
    ]
    loads.append(pltpu.make_async_copy(tiles_hbm, tiles.at[pl.ds(0, KMAX)], load_sem.at[2]))
    for copy in loads:
        copy.start()

    barrier = pltpu.get_barrier_semaphore()
    greeted = [following, previous, partner] + y_peers + x_peers + z_peers
    for peer in greeted:
        pl.semaphore_signal(barrier, inc=1, device_id=peer, device_id_type=MESH)
    tiles[KMAX] = jnp.zeros((TILE, TILE), F32)
    loads[0].wait()
    loads[1].wait()
    pl.semaphore_wait(barrier, len(greeted))

    band_copy = {}

    def band_send(s, c):
        band_copy[s, c] = send(
            band.at[s, c], band.at[s + 1, c], band_s.at[s, c], band_r.at[s, c], following
        )

    def band_take(s, c):
        high, low = split(band[s, c])
        x_cat[c, s * ROWS:(s + 1) * ROWS, 0:HALF] = high
        x_cat[c, s * ROWS:(s + 1) * ROWS, HALF:2 * HALF] = low

    def band_step(s, c):
        band_copy[s, c].wait_recv()
        if s + 1 < STOPS - 1:
            band_send(s + 1, c)
        band_take(s + 1, c)

    band_send(0, 0)
    band_send(0, 1)
    band_take(0, 0)
    band_take(0, 1)
    loads[2].wait()

    def fill_rows(d, carry):
        for half in range(2):
            for q in range(8):
                tile = tiles[inv[(d * 2 + half) * 8 + q]]
                high, low = split(tile)
                a_hi[d, half * TILE:(half + 1) * TILE, q * TILE:(q + 1) * TILE] = high
                a_lo[d, half * TILE:(half + 1) * TILE, q * TILE:(q + 1) * TILE] = low
        return carry

    def fill_turned(i, carry):
        xq = i // STOPS
        s = lax.rem(i, STOPS)
        for tt in range(4):
            for j in range(2):
                tile = tiles[inv[(xq * 4 + tt) * 8 + s * 2 + j]]
                high, low = split(tile.T)
                t_hi[xq, s, j * TILE:(j + 1) * TILE, tt * TILE:(tt + 1) * TILE] = high
                t_lo[xq, s, j * TILE:(j + 1) * TILE, tt * TILE:(tt + 1) * TILE] = low
        return carry

    def turn(part):
        lax.fori_loop(part * 4, part * 4 + 4, fill_turned, 0)

    lax.fori_loop(0, 2, fill_rows, 0)
    band_step(0, 0)
    lax.fori_loop(2, 4, fill_rows, 0)
    band_step(0, 1)
    lax.fori_loop(4, 6, fill_rows, 0)
    band_step(1, 0)
    lax.fori_loop(6, 8, fill_rows, 0)
    band_step(1, 1)
    band_step(2, 0)

    units = [(0, 0), (0, 1), (1, 0), (1, 1)]
    rs_copy = {}

    def partial_rows(u, place, x_to):
        own, c = units[u]
        d = x_to * 2 + (z_hi if own else 1 - z_hi)
        both = dot(a_hi[d], x_cat[c])
        rest = dot(a_lo[d], x_cat[c, :, 0:HALF])
        pbuf[u, place] = both[:, 0:HALF] + (both[:, HALF:2 * HALF] + rest)

    upper = pl.ds(0, HALF)
    lower = pl.ds(HALF, HALF)

    def rs_send(u, k, src, dst, to):
        rs_copy[u, k] = send(src, dst, rs_s.at[u, k], rs_r.at[u, k], to)

    def rs_begin(u):
        partial_rows(u, 0, x_opp)
        rs_send(u, 0, pbuf.at[u, 0, upper], rx1.at[u, 0], right)
        rs_send(u, 1, pbuf.at[u, 0, lower], rx1.at[u, 1], left)
        partial_rows(u, 1, x_right)
        rs_send(u, 2, pbuf.at[u, 1, lower], rx2.at[u, 0, lower], right)
        partial_rows(u, 2, x_left)
        rs_send(u, 3, pbuf.at[u, 2, upper], rx2.at[u, 1, upper], left)
        partial_rows(u, 3, x)

    def rs_relay(u):
        rs_copy[u, 0].wait_recv()
        pbuf[u, 1, upper] = pbuf[u, 1, upper] + rx1[u, 0]
        rs_send(u, 4, pbuf.at[u, 1, upper], rx2.at[u, 0, upper], right)
        rs_copy[u, 1].wait_recv()
        pbuf[u, 2, lower] = pbuf[u, 2, lower] + rx1[u, 1]
        rs_send(u, 5, pbuf.at[u, 2, lower], rx2.at[u, 1, lower], left)

    zx_copy = {}

    def rs_finish(u):
        own, c = units[u]
        for k in (2, 3, 4, 5):
            rs_copy[u, k].wait_recv()
        total = pbuf[u, 3] + (rx2[u, 0] + rx2[u, 1])
        if own:
            zx_copy[c].wait_recv()
            mine[:, c * HALF:(c + 1) * HALF] = total + zrecv[c]
        else:
            zsend[c] = total
            zx_copy[c] = send(zsend.at[c], zrecv.at[c], zx_s.at[c], zx_r.at[c], across)

    rs_begin(0)
    band_step(2, 1)
    rs_begin(1)
    rs_relay(0)
    turn(0)
    rs_begin(2)
    rs_relay(1)
    rs_finish(0)
    turn(1)
    rs_begin(3)
    rs_relay(2)
    rs_finish(1)
    turn(2)
    rs_relay(3)
    turn(3)
    w_parts = split(weight[...])
    rs_finish(2)
    rs_finish(3)

    total = mine[...]
    preact = dot3(split(total), w_parts)
    squashed = jax.nn.sigmoid(preact)
    act[...] = preact * squashed
    slopes = cot[...] * squashed * (1.0 + preact * (1.0 - squashed))
    s_parts = split(slopes)

    ag_copy = {}
    az_copy = {}

    def ag_send(own, c, k, src, to):
        ag_copy[own, c, k] = send(src, src, ag_s.at[own, c, k], ag_r.at[own, c, k], to)

    for c in range(2):
        w_rows = (w_parts[0][c * HALF:(c + 1) * HALF, :], w_parts[1][c * HALF:(c + 1) * HALF, :])
        g[rep, c] = dot3(s_parts, w_rows, ((1,), (1,)))
        block = g.at[rep, c]
        az_copy[c] = send(block, block, az_s.at[c], az_r.at[c], across)
        ag_send(1, c, 0, block, right)
        ag_send(1, c, 1, block, left)

    red_copy = {}

    def red_send(k, src, dst, to):
        red_copy[k] = send(src, dst, red_s.at[k], red_r.at[k], to)

    turned = split(total.T)
    for c in range(2):
        lw[c] = dot3(turned, (s_parts[0][:, c * HALF:(c + 1) * HALF], s_parts[1][:, c * HALF:(c + 1) * HALF]))
    red_send(0, lw.at[1 - core], cr, partner)

    def red_y():
        red_copy[0].wait_recv()
        lw[core] = lw[core] + cr[...]
        for k in range(1, NY):
            rows = pl.ds(pl.multiple_of(lax.rem(y + k, NY) * 32, 32), 32)
            red_send(k, lw.at[core, rows], yr.at[y], y_peers[k - 1])
        yr[y] = lw[core, pl.ds(pl.multiple_of(y * 32, 32), 32)]

    def red_x():
        for k in range(1, NY):
            red_copy[k].wait_recv()
        yr[0] = jnp.sum(yr[...], axis=0)
        for k in range(1, NX):
            rows = pl.ds(pl.multiple_of(lax.rem(x + k, NX) * 8, 8), 8)
            red_send(7 + k, yr.at[0, rows], xr.at[x], x_peers[k - 1])
        xr[x] = yr[0, pl.ds(pl.multiple_of(x * 8, 8), 8)]

    def red_z():
        for k in range(1, NX):
            red_copy[7 + k].wait_recv()
        zz[z] = jnp.sum(xr[...], axis=0)
        for k in range(1, NZ):
            red_send(10 + k, zz.at[z], zz.at[z], z_peers[k - 1])

    def red_x_back():
        for k in range(1, NZ):
            red_copy[10 + k].wait_recv()
        rows = pl.ds(pl.multiple_of(y * 32 + x * 8, 8), 8)
        wh[rows] = jnp.sum(zz[...], axis=0) * (1.0 / math.sqrt(SLABS * 8 * ROWS))
        for k in range(1, NX):
            red_send(17 + k, wh.at[rows], wh.at[rows], x_peers[k - 1])

    def red_y_back():
        for k in range(1, NX):
            red_copy[17 + k].wait_recv()
        rows = pl.ds(pl.multiple_of(y * 32, 32), 32)
        for k in range(1, NY):
            red_send(20 + k, wh.at[rows], wh.at[rows], y_peers[k - 1])

    def red_core_back():
        for k in range(1, NY):
            red_copy[20 + k].wait_recv()
        gwb[core] = wh[...]
        red_send(28, gwb.at[core], gwb.at[core], partner)

    def ag_relay(own, c):
        w = z_hi if own else 1 - z_hi
        ag_copy[own, c, 0].wait_recv()
        ag_send(own, c, 2, g.at[x_left * 2 + w, c, upper], right)
        ag_copy[own, c, 1].wait_recv()
        ag_send(own, c, 3, g.at[x_right * 2 + w, c, lower], left)

    def ag_across(c):
        az_copy[c].wait_recv()
        block = g.at[x * 2 + 1 - z_hi, c]
        ag_send(0, c, 0, block, right)
        ag_send(0, c, 1, block, left)

    def ag_last(c):
        for own in range(2):
            for k in (2, 3):
                ag_copy[own, c, k].wait_recv()

    def spread(xq, c, first=False):
        for j in range(2):
            high, low = split(g[xq * 2 + j, c])
            x_cat[c, j * ROWS:(j + 1) * ROWS, 0:HALF] = high
            x_cat[c, j * ROWS:(j + 1) * ROWS, HALF:2 * HALF] = low

        def one_stop(s, carry):
            both = dot(t_hi[xq, s], x_cat[c, 0:2 * ROWS])
            rest = dot(t_lo[xq, s], x_cat[c, 0:2 * ROWS, 0:HALF])
            term = both[:, 0:HALF] + (both[:, HALF:2 * HALF] + rest)
            sp[c, s] = term if first else sp[c, s] + term
            return carry

        lax.fori_loop(0, STOPS, one_stop, 0)

    ring_copy = {}

    def ring_send(c, step):
        ring_copy[c, step] = send(
            sp.at[c, STOPS - 1 - step], rr.at[step, c], ring_s.at[c, step], ring_r.at[c, step],
            previous,
        )

    def ring_step(c, step):
        ring_copy[c, step].wait_recv()
        s = STOPS - 2 - step
        if s > 0:
            sp[c, s] = sp[c, s] + rr[step, c]
            ring_send(c, step + 1)
        else:
            gf[:, c * HALF:(c + 1) * HALF] = sp[c, 0] + rr[step, c]

    ag_relay(1, 0)
    ag_across(0)
    red_y()
    ag_relay(1, 1)
    ag_across(1)
    spread(x, 0, first=True)
    spread(x, 1, first=True)
    red_x()
    ag_relay(0, 0)
    spread(x_right, 0)
    spread(x_left, 0)
    red_z()
    ag_relay(0, 1)
    spread(x_right, 1)
    spread(x_left, 1)
    red_x_back()
    ag_last(0)
    spread(x_opp, 0)
    ring_send(0, 0)
    red_y_back()
    ag_last(1)
    spread(x_opp, 1)
    ring_send(1, 0)
    ring_step(0, 0)
    red_core_back()
    ring_step(1, 0)
    ring_step(0, 1)
    ring_step(1, 1)
    ring_step(0, 2)
    ring_step(1, 2)
    red_copy[28].wait_recv()
    gw[:, 0:HALF] = gwb[0]
    gw[:, HALF:2 * HALF] = gwb[1]
    for copy in started:
        copy.wait_send()


def layer(inv, features, weight, cotangent, tiles):
    vmem = pl.BlockSpec(memory_space=pltpu.VMEM)
    hbm = pl.BlockSpec(memory_space=pl.ANY)
    dma = lambda *shape: pltpu.SemaphoreType.DMA(shape)
    block = (ROWS, HALF)
    scratch = [
        pltpu.VMEM((KMAX + 1, TILE, TILE), F32),
        pltpu.VMEM((8, ROWS, STOPS * ROWS), BF),
        pltpu.VMEM((8, ROWS, STOPS * ROWS), BF),
        pltpu.VMEM((NX, STOPS, ROWS, 2 * ROWS), BF),
        pltpu.VMEM((NX, STOPS, ROWS, 2 * ROWS), BF),
        pltpu.VMEM((STOPS, 2) + block, F32),
        pltpu.VMEM((2, STOPS * ROWS, 2 * HALF), BF),
        pltpu.VMEM((4, 4) + block, F32),
        pltpu.VMEM((4, 2, HALF, HALF), F32),
        pltpu.VMEM((4, 2) + block, F32),
        pltpu.VMEM((2,) + block, F32),
        pltpu.VMEM((2,) + block, F32),
        pltpu.VMEM((ROWS, HID), F32),
        pltpu.VMEM((8, 2) + block, F32),
        pltpu.VMEM((2, STOPS) + block, F32),
        pltpu.VMEM((STOPS - 1, 2) + block, F32),
        pltpu.VMEM((2,) + block, F32),
        pltpu.VMEM(block, F32),
        pltpu.VMEM((NY, 32, HALF), F32),
        pltpu.VMEM((NX, 8, HALF), F32),
        pltpu.VMEM((NZ, 8, HALF), F32),
        pltpu.VMEM(block, F32),
        pltpu.VMEM((2,) + block, F32),
        dma(3),
        dma(3, 2), dma(3, 2),
        dma(4, 6), dma(4, 6),
        dma(2), dma(2),
        dma(2, 2, 4), dma(2, 2, 4),
        dma(2), dma(2),
        dma(2, 3), dma(2, 3),
        dma(29), dma(29),
    ]
    return pl.pallas_call(
        kernel,
        out_shape=(
            jax.ShapeDtypeStruct((ROWS, HID), F32),
            jax.ShapeDtypeStruct((ROWS, HID), F32),
            jax.ShapeDtypeStruct((HID, HID), F32),
        ),
        in_specs=[pl.BlockSpec(memory_space=pltpu.SMEM), hbm, vmem, vmem, hbm],
        out_specs=(vmem, vmem, vmem),
        scratch_shapes=scratch,
        compiler_params=pltpu.CompilerParams(
            collective_id=0, has_side_effects=True, vmem_limit_bytes=48 << 20
        ),
        name="graph_layer",
    )(inv, features, weight, cotangent, tiles)


def body(features, weight, cotangent, tile_values, tile_pos, tile_count):
    pos_here = tile_pos[0, 0]
    slots = jnp.arange(KMAX, dtype=jnp.int32)
    live = slots < tile_count[0, 0]
    places = jnp.arange(TILE, dtype=jnp.int32)
    hit = (pos_here[None, :] == places[:, None]) & live[None, :]
    inv = KMAX + jnp.sum(jnp.where(hit, slots[None, :] - KMAX, 0), axis=1)
    return layer(inv, features, weight, cotangent, tile_values[0, 0])


def solution(mesh):
    in_specs = (
        P(("row", "rep"), None),
        P(),
        P(("row", "rep"), None),
        P("row", "rep", None, None, None),
        P("row", "rep", None),
        P("row", "rep"),
    )
    out_specs = (P(("row", "rep"), None), P(("row", "rep"), None), P())
    return jax.shard_map(body, mesh=mesh, in_specs=in_specs, out_specs=out_specs, check_vma=False)
```

```python
import functools
import math

import jax
import jax.numpy as jnp
from jax import lax
from jax.experimental import pallas as pl
from jax.experimental.pallas import tpu as pltpu
from jax.sharding import PartitionSpec as P

HID = 256
TILE = 128
STOPS = 4
KMAX = 40
ROWS = 256
HALF = 128
NX = 4
NY = 8
NZ = 8
SLABS = 64
MESH = pl.DeviceIdType.MESH
BF = jnp.bfloat16
F32 = jnp.float32


def split(value):
    high = value.astype(BF)
    low = (value - high.astype(F32)).astype(BF)
    return high, low


def dot(a, b, contract=((1,), (0,))):
    return lax.dot_general(a, b, (contract, ((), ())), preferred_element_type=F32)


def dot3(a, b, contract=((1,), (0,))):
    a_hi, a_lo = a
    b_hi, b_lo = b
    return dot(a_hi, b_hi, contract) + (dot(a_hi, b_lo, contract) + dot(a_lo, b_hi, contract))


def kernel(
    pos, count, feat, weight_hbm, cot_hbm, tiles_hbm, act_hbm, gf_hbm, gw_hbm,
    act, gf, tiles, inv_row, inv, weight, w_hi, w_lo, cot, slopes, a_hi, a_lo, t_hi, t_lo, band, x_cat,
    pbuf, rx1, rx2, zsend, zrecv, mine, g, sp, rr, lw, cr, yr, xr, zz, wh, gwb,
    load_sem, store_sem, band_s, band_r, rs_s, rs_r, zx_s, zx_r, ag_s, ag_r, az_s, az_r,
    ring_s, ring_r, red_s, red_r,
):
    row = lax.axis_index("row")
    rep = lax.axis_index("rep")
    core = lax.rem(row, 2)
    y = lax.rem(row // 2, NY)
    z_lo = row // 16
    x = rep // 2
    z_hi = lax.rem(rep, 2)
    z = z_hi * 4 + z_lo

    def device(core_, y_, z_, x_):
        return (lax.rem(z_, 4) * 16 + y_ * 2 + core_, x_ * 2 + z_ // 4)

    x_right = lax.rem(x + 1, NX)
    x_opp = lax.rem(x + 2, NX)
    x_left = lax.rem(x + 3, NX)
    right = (row, x_right * 2 + z_hi)
    left = (row, x_left * 2 + z_hi)
    across = (row, x * 2 + 1 - z_hi)
    partner = (row + 1 - 2 * core, rep)
    following = (lax.rem(row + 1, SLABS), rep)
    previous = (lax.rem(row + SLABS - 1, SLABS), rep)
    y_peers = [device(core, lax.rem(y + k, NY), z, x) for k in range(1, NY)]
    x_peers = [device(core, y, z, lax.rem(x + k, NX)) for k in range(1, NX)]
    z_peers = [device(core, y, lax.rem(z + k, NZ), x) for k in range(1, NZ)]

    started = []
    stores = []

    def store(src, dst, k):
        copy = pltpu.make_async_copy(src, dst, store_sem.at[k])
        copy.start()
        stores.append(copy)

    def send(src, dst, s_sem, r_sem, to):
        copy = pltpu.make_async_remote_copy(
            src_ref=src, dst_ref=dst, send_sem=s_sem, recv_sem=r_sem,
            device_id=to, device_id_type=MESH,
        )
        copy.start()
        started.append(copy)
        return copy

    barrier = pltpu.get_barrier_semaphore()
    greeted = [following, previous, partner] + y_peers + x_peers + z_peers
    for peer in greeted:
        pl.semaphore_signal(barrier, inc=1, device_id=peer, device_id_type=MESH)

    loads = [
        pltpu.make_async_copy(tiles_hbm.at[0, 0], tiles.at[pl.ds(0, KMAX)], load_sem.at[0]),
        pltpu.make_async_copy(feat.at[:, pl.ds(0, HALF)], band.at[0, 0], load_sem.at[1]),
        pltpu.make_async_copy(feat.at[:, pl.ds(HALF, HALF)], band.at[0, 1], load_sem.at[2]),
        pltpu.make_async_copy(weight_hbm, weight, load_sem.at[3]),
        pltpu.make_async_copy(cot_hbm, cot, load_sem.at[4]),
    ]
    for copy in loads:
        copy.start()

    lanes = lax.broadcasted_iota(jnp.int32, (1, TILE), 1)
    found = jnp.full((1, TILE), KMAX, jnp.int32)
    for k in range(KMAX):
        place = jnp.where(k < count[0, 0], pos[0, 0, k], -1)
        found = jnp.where(lanes == place, k, found)
    inv_row[...] = found
    to_scalars = pltpu.make_async_copy(inv_row, inv, load_sem.at[5])
    to_scalars.start()
    tiles[KMAX] = jnp.zeros((TILE, TILE), F32)
    pl.semaphore_wait(barrier, len(greeted))

    band_copy = {}

    def band_send(s, c):
        for h in range(2):
            rows = pl.ds(h * HALF, HALF)
            src = band.at[s, c, rows] if s > 0 else feat.at[rows, pl.ds(c * HALF, HALF)]
            band_copy[s, c, h] = send(
                src, band.at[s + 1, c, rows], band_s.at[s, c, h], band_r.at[s, c, h], following
            )

    def band_take(s, c):
        high, low = split(band[s, c])
        x_cat[c, s * ROWS:(s + 1) * ROWS, 0:HALF] = high
        x_cat[c, s * ROWS:(s + 1) * ROWS, HALF:2 * HALF] = low

    def band_step(s, c):
        for h in range(2):
            band_copy[s, c, h].wait_recv()
            if s + 1 < STOPS - 1:
                rows = pl.ds(h * HALF, HALF)
                band_copy[s + 1, c, h] = send(
                    band.at[s + 1, c, rows], band.at[s + 2, c, rows],
                    band_s.at[s + 1, c, h], band_r.at[s + 1, c, h], following,
                )
        band_take(s + 1, c)

    band_send(0, 0)
    to_scalars.wait()
    for copy in loads[:3]:
        copy.wait()
    band_take(0, 0)
    band_take(0, 1)

    def fill_rows(x_at, own, half):
        d = x_at * 2 + (z_hi if own else 1 - z_hi)
        for q in range(8):
            tile = tiles[inv[0, (d * 2 + half) * 8 + q]]
            high, low = split(tile)
            a_hi[d, half * TILE:(half + 1) * TILE, q * TILE:(q + 1) * TILE] = high
            a_lo[d, half * TILE:(half + 1) * TILE, q * TILE:(q + 1) * TILE] = low

    def fill_all(own, half):
        def one(i, carry):
            fill_rows(lax.rem(x + i, NX), own, half)
            return carry

        lax.fori_loop(0, NX, one, 0)

    def fill_turned(i, carry):
        d = i // STOPS
        s = lax.rem(i, STOPS)
        for tt in range(2):
            for j in range(2):
                tile = tiles[inv[0, (d * 2 + tt) * 8 + s * 2 + j]]
                high, low = split(tile.T)
                t_hi[d, s, j * TILE:(j + 1) * TILE, tt * TILE:(tt + 1) * TILE] = high
                t_lo[d, s, j * TILE:(j + 1) * TILE, tt * TILE:(tt + 1) * TILE] = low
        return carry

    def turn(part):
        lax.fori_loop(part * 8, part * 8 + 8, fill_turned, 0)

    fill_all(0, 0)
    band_step(0, 0)
    band_send(0, 1)
    fill_all(0, 1)
    band_step(1, 0)
    band_step(0, 1)
    band_step(2, 0)

    rs_copy = {}

    def partial_rows(u, place, x_to, c):
        own, half = u // 2, u % 2
        d = x_to * 2 + (z_hi if own else 1 - z_hi)
        rows = pl.ds(half * HALF, HALF)
        both = dot(a_hi[d, rows], x_cat[c])
        rest = dot(a_lo[d, rows], x_cat[c, :, 0:HALF])
        pbuf[u, place, c] = both[:, 0:HALF] + (both[:, HALF:2 * HALF] + rest)

    def rs_send(u, k, src, dst, to):
        rs_copy[u, k] = send(src, dst, rs_s.at[u, k], rs_r.at[u, k], to)

    def rs_begin(u, c):
        partial_rows(u, 0, x_opp, c)
        if c == 0:
            rs_send(u, 0, pbuf.at[u, 0, 0], rx1.at[u, 0], right)
            partial_rows(u, 2, x_left, 0)
            rs_send(u, 2, pbuf.at[u, 2, 0], rx2.at[u, 1, 0], left)
            partial_rows(u, 1, x_right, 0)
        else:
            rs_send(u, 1, pbuf.at[u, 0, 1], rx1.at[u, 1], left)
            partial_rows(u, 1, x_right, 1)
            rs_send(u, 3, pbuf.at[u, 1, 1], rx2.at[u, 0, 1], right)
            partial_rows(u, 2, x_left, 1)
        partial_rows(u, 3, x, c)

    def rs_relay(u, c):
        rs_copy[u, c].wait_recv()
        place, to = (1, right) if c == 0 else (2, left)
        pbuf[u, place, c] = pbuf[u, place, c] + rx1[u, c]
        rs_send(u, 4 + c, pbuf.at[u, place, c], rx2.at[u, c, c], to)

    zx_copy = {}

    def rs_finish(u):
        own, half = u // 2, u % 2
        for k in (2, 3, 4, 5):
            rs_copy[u, k].wait_recv()
        if own:
            zx_copy[half].wait_recv()
        for c in range(2):
            total = pbuf[u, 3, c] + (rx2[u, 0, c] + rx2[u, 1, c])
            if own:
                mine[half * HALF:(half + 1) * HALF, c * HALF:(c + 1) * HALF] = total + zrecv[half, c]
            else:
                zsend[half, c] = total
        if not own:
            zx_copy[half] = send(
                zsend.at[half], zrecv.at[half], zx_s.at[half], zx_r.at[half], across
            )

    ag_copy = {}
    az_copy = {}
    taken = set()

    def place_of(own, x_at):
        return x_at * 2 + (z_hi if own else 1 - z_hi)

    def ag_send(own, h, c, k, src, to):
        ag_copy[own, h, c, k] = send(src, src, ag_s.at[own, h, c, k], ag_r.at[own, h, c, k], to)

    def ag_take(own, h, c, k):
        if (own, h, c, k) not in taken:
            taken.add((own, h, c, k))
            ag_copy[own, h, c, k].wait_recv()

    def ag_relay(own, h, c):
        if (c if own else h) == 0:
            ag_take(own, h, c, 0)
            ag_send(own, h, c, 2, g.at[place_of(own, x_left), h, c], right)
        else:
            ag_take(own, h, c, 1)
            ag_send(own, h, c, 2, g.at[place_of(own, x_right), h, c], left)

    def ag_across(h, c):
        az_copy[h, c].wait_recv()
        block = g.at[place_of(0, x), h, c]
        ag_send(0, h, c, 0, block, right)
        ag_send(0, h, c, 1, block, left)

    def share_rows(h):
        rows = pl.ds(h * HALF, HALF)
        preact = dot3(split(mine[rows, :]), (w_hi[...], w_lo[...]))
        squashed = jax.nn.sigmoid(preact)
        slope = cot[rows, :] * squashed * (1.0 + preact * (1.0 - squashed))
        s_parts = split(slope)
        for c in range(2):
            columns = slice(c * HALF, (c + 1) * HALF)
            g[rep, h, c] = dot3(s_parts, (w_hi[columns, :], w_lo[columns, :]), ((1,), (1,)))
            block = g.at[rep, h, c]
            az_copy[h, c] = send(block, block, az_s.at[h, c], az_r.at[h, c], across)
            if c == 0:
                ag_send(1, h, 0, 0, block, right)
        ag_send(1, h, 1, 1, g.at[rep, h, 1], left)
        ag_send(1, h, 1, 0, g.at[rep, h, 1], right)
        ag_send(1, h, 0, 1, g.at[rep, h, 0], left)
        act[rows, :] = preact * squashed
        store(act.at[rows], act_hbm.at[rows], h)
        slopes[rows, :] = slope

    rs_begin(0, 0)
    band_step(1, 1)
    rs_begin(1, 0)
    band_step(2, 1)
    rs_begin(0, 1)
    rs_relay(0, 0)
    rs_begin(1, 1)
    rs_relay(0, 1)
    rs_relay(1, 0)
    fill_all(1, 0)
    rs_relay(1, 1)
    rs_begin(2, 0)
    rs_begin(2, 1)
    rs_finish(0)
    fill_all(1, 1)
    rs_relay(2, 0)
    rs_relay(2, 1)
    rs_begin(3, 0)
    rs_finish(1)
    rs_begin(3, 1)
    loads[3].wait()
    loads[4].wait()
    w_hi[...], w_lo[...] = split(weight[...])
    turn(0)
    rs_relay(3, 0)
    rs_relay(3, 1)
    rs_finish(2)
    share_rows(0)
    turn(1)
    turn(2)
    rs_finish(3)
    ag_relay(1, 0, 0)
    ag_relay(1, 0, 1)
    share_rows(1)

    red_copy = {}

    def red_send(k, src, dst, to):
        red_copy[k] = send(src, dst, red_s.at[k], red_r.at[k], to)

    turned = split(mine[...].T)
    s_parts = split(slopes[...])
    for c in range(2):
        lw[c] = dot3(turned, (s_parts[0][:, c * HALF:(c + 1) * HALF], s_parts[1][:, c * HALF:(c + 1) * HALF]))
    red_send(0, lw.at[1 - core], cr, partner)
    turn(3)

    def red_y():
        red_copy[0].wait_recv()
        lw[core] = lw[core] + cr[...]
        for k in range(1, NY):
            rows = pl.ds(pl.multiple_of(lax.rem(y + k, NY) * 32, 32), 32)
            red_send(k, lw.at[core, rows], yr.at[y], y_peers[k - 1])
        yr[y] = lw[core, pl.ds(pl.multiple_of(y * 32, 32), 32)]

    def red_x():
        for k in range(1, NY):
            red_copy[k].wait_recv()
        yr[0] = jnp.sum(yr[...], axis=0)
        for k in range(1, NX):
            rows = pl.ds(pl.multiple_of(lax.rem(x + k, NX) * 8, 8), 8)
            red_send(7 + k, yr.at[0, rows], xr.at[x], x_peers[k - 1])
        xr[x] = yr[0, pl.ds(pl.multiple_of(x * 8, 8), 8)]

    def red_z():
        for k in range(1, NX):
            red_copy[7 + k].wait_recv()
        zz[z] = jnp.sum(xr[...], axis=0)
        for k in range(1, NZ):
            red_send(10 + k, zz.at[z], zz.at[z], z_peers[k - 1])

    def red_x_back():
        for k in range(1, NZ):
            red_copy[10 + k].wait_recv()
        rows = pl.ds(pl.multiple_of(y * 32 + x * 8, 8), 8)
        wh[rows] = jnp.sum(zz[...], axis=0) * (1.0 / math.sqrt(SLABS * 8 * ROWS))
        for k in range(1, NX):
            red_send(17 + k, wh.at[rows], wh.at[rows], x_peers[k - 1])

    def red_y_back():
        for k in range(1, NX):
            red_copy[17 + k].wait_recv()
        rows = pl.ds(pl.multiple_of(y * 32, 32), 32)
        for k in range(1, NY):
            red_send(20 + k, wh.at[rows], wh.at[rows], y_peers[k - 1])

    def red_core_back():
        for k in range(1, NY):
            red_copy[20 + k].wait_recv()
        gwb[core] = wh[...]
        red_send(28, gwb.at[core], gwb.at[core], partner)

    def spread_begin(d, c):
        for h in range(2):
            rows = slice(h * HALF, (h + 1) * HALF)
            high, low = split(g[d, h, c])
            x_cat[c, rows, 0:HALF] = high
            x_cat[c, rows, HALF:2 * HALF] = low

    def spread_stop(d, c, s, first=False):
        both = dot(t_hi[d, s], x_cat[c, 0:ROWS])
        rest = dot(t_lo[d, s], x_cat[c, 0:ROWS, 0:HALF])
        term = both[:, 0:HALF] + (both[:, HALF:2 * HALF] + rest)
        sp[c, s] = term if first else sp[c, s] + term

    def spread(own, x_at, c, first=False):
        d = place_of(own, x_at)
        spread_begin(d, c)

        def one_stop(s, carry):
            spread_stop(d, c, s, first)
            return carry

        lax.fori_loop(0, STOPS, one_stop, 0)

    def spread_sides(own, c):
        for k, x_at in ((1, x_right), (0, x_left)):
            for h in range(2):
                ag_take(own, h, c, k)
            spread(own, x_at, c)

    def spread_opposite(own, c):
        for h in range(2):
            ag_take(own, h, c, 2)
        if own:
            spread(own, x_opp, c)
            return
        d = place_of(own, x_opp)
        spread_begin(d, c)
        spread_stop(d, c, STOPS - 1)
        ring_send(c, 0, 0)
        ring_send(c, 0, 1)

        def one_stop(i, carry):
            spread_stop(d, c, STOPS - 2 - i)
            return carry

        lax.fori_loop(0, STOPS - 1, one_stop, 0)

    ring_copy = {}

    def ring_send(c, step, h):
        rows = pl.ds(h * HALF, HALF)
        ring_copy[c, step, h] = send(
            sp.at[c, STOPS - 1 - step, rows], rr.at[step, c, rows],
            ring_s.at[c, step, h], ring_r.at[c, step, h], previous,
        )

    def ring_step(c, step):
        s = STOPS - 2 - step
        for h in range(2):
            ring_copy[c, step, h].wait_recv()
            rows = pl.ds(h * HALF, HALF)
            if s > 0:
                sp[c, s, rows] = sp[c, s, rows] + rr[step, c, rows]
                ring_send(c, step + 1, h)
            else:
                gf[c, rows] = sp[c, 0, rows] + rr[step, c, rows]
        if s == 0:
            store(gf.at[c], gf_hbm.at[:, pl.ds(c * HALF, HALF)], 2 + c)

    ag_across(0, 0)
    spread(1, x, 0, first=True)
    ag_relay(1, 1, 0)
    ag_relay(1, 1, 1)
    red_y()
    spread(1, x, 1, first=True)
    ag_across(0, 1)
    spread_sides(1, 0)
    ag_relay(0, 0, 0)
    spread_sides(1, 1)
    ag_across(1, 0)
    spread(0, x, 0)
    spread_opposite(1, 0)
    ag_relay(0, 0, 1)
    red_x()
    spread_opposite(1, 1)
    ag_across(1, 1)
    ag_relay(0, 1, 0)
    spread(0, x, 1)
    spread_sides(0, 0)
    ag_relay(0, 1, 1)
    spread_opposite(0, 0)
    red_z()
    spread_sides(0, 1)
    ring_step(0, 0)
    spread_opposite(0, 1)
    red_x_back()
    ring_step(0, 1)
    ring_step(1, 0)
    red_y_back()
    ring_step(0, 2)
    ring_step(1, 1)
    red_core_back()
    ring_step(1, 2)
    red_copy[28].wait_recv()
    for c in range(2):
        store(gwb.at[c], gw_hbm.at[:, pl.ds(c * HALF, HALF)], 4 + c)
    for copy in stores:
        copy.wait()
    for copy in started:
        copy.wait_send()


def write_out(act, gf, gw, act_out, gf_out, gw_out, held, sems):
    for first, refs in ((0, (act, gf, gw)), (3, (act_out, gf_out, gw_out))):
        copies = [
            pltpu.make_async_copy(ref, held.at[i], sems.at[first + i])
            if first == 0
            else pltpu.make_async_copy(held.at[i], ref, sems.at[first + i])
            for i, ref in enumerate(refs)
        ]
        for copy in copies:
            copy.start()
        for copy in copies:
            copy.wait()


def layer(pos, count, features, weight, cotangent, tiles):
    smem = pl.BlockSpec(memory_space=pltpu.SMEM)
    hbm = pl.BlockSpec(memory_space=pltpu.HBM)
    dma = lambda *shape: pltpu.SemaphoreType.DMA(shape)
    block = (ROWS, HALF)
    piece = (HALF, HALF)
    scratch = [
        pltpu.VMEM((ROWS, HID), F32),
        pltpu.VMEM((2,) + block, F32),
        pltpu.VMEM((KMAX + 1, TILE, TILE), F32),
        pltpu.VMEM((1, TILE), jnp.int32),
        pltpu.SMEM((1, TILE), jnp.int32),
        pltpu.VMEM((HID, HID), F32),
        pltpu.VMEM((HID, HID), BF),
        pltpu.VMEM((HID, HID), BF),
        pltpu.VMEM((ROWS, HID), F32),
        pltpu.VMEM((ROWS, HID), F32),
        pltpu.VMEM((8, ROWS, STOPS * ROWS), BF),
        pltpu.VMEM((8, ROWS, STOPS * ROWS), BF),
        pltpu.VMEM((8, STOPS, ROWS, ROWS), BF),
        pltpu.VMEM((8, STOPS, ROWS, ROWS), BF),
        pltpu.VMEM((STOPS, 2) + block, F32),
        pltpu.VMEM((2, STOPS * ROWS, 2 * HALF), BF),
        pltpu.VMEM((4, 4, 2) + piece, F32),
        pltpu.VMEM((4, 2) + piece, F32),
        pltpu.VMEM((4, 2, 2) + piece, F32),
        pltpu.VMEM((2, 2) + piece, F32),
        pltpu.VMEM((2, 2) + piece, F32),
        pltpu.VMEM((ROWS, HID), F32),
        pltpu.VMEM((8, 2, 2) + piece, F32),
        pltpu.VMEM((2, STOPS) + block, F32),
        pltpu.VMEM((STOPS - 1, 2) + block, F32),
        pltpu.VMEM((2,) + block, F32),
        pltpu.VMEM(block, F32),
        pltpu.VMEM((NY, 32, HALF), F32),
        pltpu.VMEM((NX, 8, HALF), F32),
        pltpu.VMEM((NZ, 8, HALF), F32),
        pltpu.VMEM(block, F32),
        pltpu.VMEM((2,) + block, F32),
        dma(6), dma(6),
        dma(3, 2, 2), dma(3, 2, 2),
        dma(4, 6), dma(4, 6),
        dma(2), dma(2),
        dma(2, 2, 2, 3), dma(2, 2, 2, 3),
        dma(2, 2), dma(2, 2),
        dma(2, 3, 2), dma(2, 3, 2),
        dma(29), dma(29),
    ]
    outs = (
        jax.ShapeDtypeStruct((ROWS, HID), F32),
        jax.ShapeDtypeStruct((ROWS, HID), F32),
        jax.ShapeDtypeStruct((HID, HID), F32),
    )
    parts = pl.pallas_call(
        kernel,
        out_shape=outs,
        in_specs=[smem, smem, hbm, hbm, hbm, hbm],
        out_specs=(hbm, hbm, hbm),
        scratch_shapes=scratch,
        compiler_params=pltpu.CompilerParams(
            collective_id=0, has_side_effects=True, vmem_limit_bytes=60 << 20
        ),
        name="graph_layer",
    )(pos, count, features, weight, cotangent, tiles)
    return pl.pallas_call(
        write_out,
        out_shape=outs,
        in_specs=[hbm, hbm, hbm],
        out_specs=(hbm, hbm, hbm),
        scratch_shapes=[pltpu.VMEM((3, ROWS, HID), F32), dma(6)],
        compiler_params=pltpu.CompilerParams(vmem_limit_bytes=60 << 20),
        name="write_out",
    )(*parts)


def body(features, weight, cotangent, tile_values, tile_pos, tile_count):
    return layer(tile_pos, tile_count, features, weight, cotangent, tile_values)


def solution(mesh):
    in_specs = (
        P(("row", "rep"), None),
        P(),
        P(("row", "rep"), None),
        P("row", "rep", None, None, None),
        P("row", "rep", None),
        P("row", "rep"),
    )
    out_specs = (P(("row", "rep"), None), P(("row", "rep"), None), P())
    return jax.shard_map(body, mesh=mesh, in_specs=in_specs, out_specs=out_specs, check_vma=False)
```

```python
import functools
import math

import jax
import jax.numpy as jnp
from jax import lax
from jax.experimental import pallas as pl
from jax.experimental.pallas import tpu as pltpu
from jax.sharding import PartitionSpec as P

HID = 256
TILE = 128
STOPS = 4
KMAX = 40
ROWS = 256
HALF = 128
BAND = STOPS * ROWS
NX = 4
NY = 8
NZ = 8
SLABS = 64
MESH = pl.DeviceIdType.MESH
BF = jnp.bfloat16
F32 = jnp.float32


def split(value):
    high = value.astype(BF)
    low = (value - high.astype(F32)).astype(BF)
    return high, low


def dot(a, b, contract=((1,), (0,))):
    return lax.dot_general(a, b, (contract, ((), ())), preferred_element_type=F32)


def dot3(a, b, contract=((1,), (0,))):
    a_hi, a_lo = a
    b_hi, b_lo = b
    return dot(a_hi, b_hi, contract) + (dot(a_hi, b_lo, contract) + dot(a_lo, b_hi, contract))


def kernel(
    pos, count, feat, weight_hbm, cot_hbm, tiles_hbm, act_hbm, gf_hbm, gw_hbm,
    act, gf, tiles, inv_row, inv, weight, w_hi, w_lo, cot, slopes, a_cat, t_cat, band, x_cat,
    pbuf, rx1, rx2, zsend, zrecv, mine, g, acc, sp, rr, lw, cr, yr, xr, zz, wh, gwb,
    load_sem, store_sem, band_s, band_r, rs_s, rs_r, zx_s, zx_r, ag_s, ag_r, az_s, az_r,
    ring_s, ring_r, red_s, red_r,
):
    row = lax.axis_index("row")
    rep = lax.axis_index("rep")
    core = lax.rem(row, 2)
    y = lax.rem(row // 2, NY)
    z_lo = row // 16
    x = rep // 2
    z_hi = lax.rem(rep, 2)
    z = z_hi * 4 + z_lo

    def device(core_, y_, z_, x_):
        return (lax.rem(z_, 4) * 16 + y_ * 2 + core_, x_ * 2 + z_ // 4)

    x_right = lax.rem(x + 1, NX)
    x_opp = lax.rem(x + 2, NX)
    x_left = lax.rem(x + 3, NX)
    right = (row, x_right * 2 + z_hi)
    left = (row, x_left * 2 + z_hi)
    across = (row, x * 2 + 1 - z_hi)
    partner = (row + 1 - 2 * core, rep)
    following = (lax.rem(row + 1, SLABS), rep)
    previous = (lax.rem(row + SLABS - 1, SLABS), rep)
    y_peers = [device(core, lax.rem(y + k, NY), z, x) for k in range(1, NY)]
    x_peers = [device(core, y, z, lax.rem(x + k, NX)) for k in range(1, NX)]
    z_peers = [device(core, y, lax.rem(z + k, NZ), x) for k in range(1, NZ)]

    started = []
    stores = []

    def store(src, dst, k):
        copy = pltpu.make_async_copy(src, dst, store_sem.at[k])
        copy.start()
        stores.append(copy)

    def send(src, dst, s_sem, r_sem, to):
        copy = pltpu.make_async_remote_copy(
            src_ref=src, dst_ref=dst, send_sem=s_sem, recv_sem=r_sem,
            device_id=to, device_id_type=MESH,
        )
        copy.start()
        started.append(copy)
        return copy

    barrier = pltpu.get_barrier_semaphore()
    greeted = [following, previous, partner] + y_peers + x_peers + z_peers
    for peer in greeted:
        pl.semaphore_signal(barrier, inc=1, device_id=peer, device_id_type=MESH)

    loads = [
        pltpu.make_async_copy(tiles_hbm.at[0, 0], tiles.at[pl.ds(0, KMAX)], load_sem.at[0]),
        pltpu.make_async_copy(feat.at[:, pl.ds(0, HALF)], band.at[0, 0], load_sem.at[1]),
        pltpu.make_async_copy(feat.at[:, pl.ds(HALF, HALF)], band.at[0, 1], load_sem.at[2]),
        pltpu.make_async_copy(weight_hbm, weight, load_sem.at[3]),
        pltpu.make_async_copy(cot_hbm, cot, load_sem.at[4]),
    ]
    for copy in loads:
        copy.start()

    lanes = lax.broadcasted_iota(jnp.int32, (1, TILE), 1)
    found = jnp.full((1, TILE), KMAX, jnp.int32)
    for k in range(KMAX):
        place = jnp.where(k < count[0, 0], pos[0, 0, k], -1)
        found = jnp.where(lanes == place, k, found)
    inv_row[...] = found
    to_scalars = pltpu.make_async_copy(inv_row, inv, load_sem.at[5])
    to_scalars.start()
    tiles[KMAX] = jnp.zeros((TILE, TILE), F32)
    pl.semaphore_wait(barrier, len(greeted))

    band_copy = {}

    def band_send(s, c):
        for h in range(2):
            rows = pl.ds(h * HALF, HALF)
            src = band.at[s, c, rows] if s > 0 else feat.at[rows, pl.ds(c * HALF, HALF)]
            band_copy[s, c, h] = send(
                src, band.at[s + 1, c, rows], band_s.at[s, c, h], band_r.at[s, c, h], following
            )

    def put_parts(c, start, value, gap):
        high, low = split(value)
        rows = value.shape[0]
        for first in (start, start + gap):
            x_cat[c, first:first + rows, 0:HALF] = high
            x_cat[c, first:first + rows, HALF:2 * HALF] = low

    def band_take(s, c):
        put_parts(c, s * ROWS, band[s, c], BAND)

    def band_step(s, c):
        for h in range(2):
            band_copy[s, c, h].wait_recv()
            if s + 1 < STOPS - 1:
                rows = pl.ds(h * HALF, HALF)
                band_copy[s + 1, c, h] = send(
                    band.at[s + 1, c, rows], band.at[s + 2, c, rows],
                    band_s.at[s + 1, c, h], band_r.at[s + 1, c, h], following,
                )
        band_take(s + 1, c)

    band_send(0, 0)
    to_scalars.wait()
    for copy in loads[:3]:
        copy.wait()
    band_take(0, 0)
    band_take(0, 1)

    def fill_rows(x_at, own, half):
        d = x_at * 2 + (z_hi if own else 1 - z_hi)
        for q in range(8):
            tile = tiles[inv[0, (d * 2 + half) * 8 + q]]
            high, low = split(tile)
            rows = slice(half * TILE, (half + 1) * TILE)
            a_cat[d, rows, q * TILE:(q + 1) * TILE] = high
            a_cat[d, rows, BAND + q * TILE:BAND + (q + 1) * TILE] = low

    def fill_all(own, half):
        def one(i, carry):
            fill_rows(lax.rem(x + i, NX), own, half)
            return carry

        lax.fori_loop(0, NX, one, 0)

    def fill_turned(i, carry):
        d = i // STOPS
        s = lax.rem(i, STOPS)
        for tt in range(2):
            for j in range(2):
                tile = tiles[inv[0, (d * 2 + tt) * 8 + s * 2 + j]]
                high, low = split(tile.T)
                rows = pl.ds(pl.multiple_of(s * ROWS + j * TILE, TILE), TILE)
                t_cat[d, rows, tt * TILE:(tt + 1) * TILE] = high
                t_cat[d, rows, ROWS + tt * TILE:ROWS + (tt + 1) * TILE] = low
        return carry

    def turn(part):
        lax.fori_loop(part * 8, part * 8 + 8, fill_turned, 0)

    fill_all(0, 0)
    band_step(0, 0)
    band_send(0, 1)
    fill_all(0, 1)
    band_step(1, 0)
    band_step(0, 1)
    band_step(2, 0)

    rs_copy = {}

    def partial_rows(u, place, x_to, c):
        d = x_to * 2 + (z_hi if u // 2 else 1 - z_hi)
        half = u % 2
        both = dot(a_cat[d, half * HALF:(half + 1) * HALF], x_cat[c])
        pbuf[u, place, c] = both[:, 0:HALF] + both[:, HALF:2 * HALF]

    def rs_send(u, k, src, dst, to):
        rs_copy[u, k] = send(src, dst, rs_s.at[u, k], rs_r.at[u, k], to)

    def rs_begin(u, c):
        partial_rows(u, 0, x_opp, c)
        if c == 0:
            rs_send(u, 0, pbuf.at[u, 0, 0], rx1.at[u, 0], right)
            partial_rows(u, 2, x_left, 0)
            rs_send(u, 2, pbuf.at[u, 2, 0], rx2.at[u, 1, 0], left)
            partial_rows(u, 1, x_right, 0)
        else:
            rs_send(u, 1, pbuf.at[u, 0, 1], rx1.at[u, 1], left)
            partial_rows(u, 1, x_right, 1)
            rs_send(u, 3, pbuf.at[u, 1, 1], rx2.at[u, 0, 1], right)
            partial_rows(u, 2, x_left, 1)
        partial_rows(u, 3, x, c)

    def rs_relay(u, c):
        rs_copy[u, c].wait_recv()
        place, to = (1, right) if c == 0 else (2, left)
        pbuf[u, place, c] = pbuf[u, place, c] + rx1[u, c]
        rs_send(u, 4 + c, pbuf.at[u, place, c], rx2.at[u, c, c], to)

    zx_copy = {}

    def rs_finish(u):
        own, half = u // 2, u % 2
        for k in (2, 3, 4, 5):
            rs_copy[u, k].wait_recv()
        if own:
            zx_copy[half].wait_recv()
        for c in range(2):
            total = pbuf[u, 3, c] + (rx2[u, 0, c] + rx2[u, 1, c])
            if own:
                mine[half * HALF:(half + 1) * HALF, c * HALF:(c + 1) * HALF] = total + zrecv[half, c]
            else:
                zsend[half, c] = total
        if not own:
            zx_copy[half] = send(
                zsend.at[half], zrecv.at[half], zx_s.at[half], zx_r.at[half], across
            )

    ag_copy = {}
    az_copy = {}
    taken = set()

    def place_of(own, x_at):
        return x_at * 2 + (z_hi if own else 1 - z_hi)

    def ag_send(own, h, c, k, src, to):
        ag_copy[own, h, c, k] = send(src, src, ag_s.at[own, h, c, k], ag_r.at[own, h, c, k], to)

    def ag_take(own, h, c, k):
        if (own, h, c, k) not in taken:
            taken.add((own, h, c, k))
            ag_copy[own, h, c, k].wait_recv()

    def ag_relay(own, h, c):
        if (c if own else h) == 0:
            ag_take(own, h, c, 0)
            ag_send(own, h, c, 2, g.at[place_of(own, x_left), h, c], right)
        else:
            ag_take(own, h, c, 1)
            ag_send(own, h, c, 2, g.at[place_of(own, x_right), h, c], left)

    def ag_across(h, c):
        az_copy[h, c].wait_recv()
        block = g.at[place_of(0, x), h, c]
        ag_send(0, h, c, 0, block, right)
        ag_send(0, h, c, 1, block, left)

    def share_rows(h):
        rows = pl.ds(h * HALF, HALF)
        preact = dot3(split(mine[rows, :]), (w_hi[...], w_lo[...]))
        squashed = jax.nn.sigmoid(preact)
        slope = cot[rows, :] * squashed * (1.0 + preact * (1.0 - squashed))
        s_parts = split(slope)
        for c in range(2):
            columns = slice(c * HALF, (c + 1) * HALF)
            g[rep, h, c] = dot3(s_parts, (w_hi[columns, :], w_lo[columns, :]), ((1,), (1,)))
            block = g.at[rep, h, c]
            az_copy[h, c] = send(block, block, az_s.at[h, c], az_r.at[h, c], across)
            if c == 0:
                ag_send(1, h, 0, 0, block, right)
        ag_send(1, h, 1, 1, g.at[rep, h, 1], left)
        ag_send(1, h, 1, 0, g.at[rep, h, 1], right)
        ag_send(1, h, 0, 1, g.at[rep, h, 0], left)
        act[rows, :] = preact * squashed
        store(act.at[rows], act_hbm.at[rows], h)
        slopes[rows, :] = slope

    rs_begin(0, 0)
    band_step(1, 1)
    rs_begin(1, 0)
    band_step(2, 1)
    rs_begin(0, 1)
    rs_relay(0, 0)
    rs_begin(1, 1)
    rs_relay(0, 1)
    rs_relay(1, 0)
    fill_all(1, 0)
    rs_relay(1, 1)
    rs_begin(2, 0)
    rs_finish(0)
    rs_begin(2, 1)
    fill_all(1, 1)
    rs_finish(1)
    rs_relay(2, 0)
    rs_relay(2, 1)
    rs_begin(3, 0)
    rs_begin(3, 1)
    loads[3].wait()
    loads[4].wait()
    w_hi[...], w_lo[...] = split(weight[...])
    turn(0)
    rs_relay(3, 0)
    rs_relay(3, 1)
    rs_finish(2)
    share_rows(0)
    turn(1)
    turn(2)
    turn(3)
    rs_finish(3)
    ag_relay(1, 0, 0)
    ag_relay(1, 0, 1)
    share_rows(1)

    red_copy = {}

    def red_send(k, src, dst, to):
        red_copy[k] = send(src, dst, red_s.at[k], red_r.at[k], to)

    turned = split(mine[...].T)
    s_parts = split(slopes[...])
    for c in range(2):
        lw[c] = dot3(turned, (s_parts[0][:, c * HALF:(c + 1) * HALF], s_parts[1][:, c * HALF:(c + 1) * HALF]))
    red_send(0, lw.at[1 - core], cr, partner)

    def red_y():
        red_copy[0].wait_recv()
        lw[core] = lw[core] + cr[...]
        for k in range(1, NY):
            rows = pl.ds(pl.multiple_of(lax.rem(y + k, NY) * 32, 32), 32)
            red_send(k, lw.at[core, rows], yr.at[y], y_peers[k - 1])
        yr[y] = lw[core, pl.ds(pl.multiple_of(y * 32, 32), 32)]

    def red_z():
        for k in range(1, NY):
            red_copy[k].wait_recv()
        zz[z] = jnp.sum(yr[...], axis=0)
        for k in range(1, NZ):
            red_send(7 + k, zz.at[z], zz.at[z], z_peers[k - 1])

    def red_x():
        for k in range(1, NZ):
            red_copy[7 + k].wait_recv()
        xr[x] = jnp.sum(zz[...], axis=0)
        for k in range(1, NX):
            red_send(14 + k, xr.at[x], xr.at[x], x_peers[k - 1])

    def red_y_back():
        for k in range(1, NX):
            red_copy[14 + k].wait_recv()
        rows = pl.ds(pl.multiple_of(y * 32, 32), 32)
        wh[rows] = jnp.sum(xr[...], axis=0) * (1.0 / math.sqrt(SLABS * 8 * ROWS))
        for k in range(1, NY):
            red_send(17 + k, wh.at[rows], wh.at[rows], y_peers[k - 1])

    def red_core_back():
        for k in range(1, NY):
            red_copy[17 + k].wait_recv()
        gwb[core] = wh[...]
        red_send(25, gwb.at[core], gwb.at[core], partner)

    def spread_begin(d, c):
        for h in range(2):
            put_parts(c, h * HALF, g[d, h, c], ROWS)

    def spread(own, x_at, c, first=False):
        d = place_of(own, x_at)
        spread_begin(d, c)

        term = dot(t_cat[d], x_cat[c, 0:2 * ROWS])
        acc[c] = term if first else acc[c] + term

    def spread_stops(d, c, low, high):
        rows = pl.ds(low * ROWS, (high - low) * ROWS)
        total = acc[c, rows] + dot(t_cat[d, rows], x_cat[c, 0:2 * ROWS])
        folded = total[:, 0:HALF] + total[:, HALF:2 * HALF]
        for s in range(low, high):
            sp[c, s] = folded[(s - low) * ROWS:(s - low + 1) * ROWS]

    def spread_sides(own, c):
        for k, x_at in ((1, x_right), (0, x_left)):
            for h in range(2):
                ag_take(own, h, c, k)
            spread(own, x_at, c)

    def spread_opposite(own, c):
        for h in range(2):
            ag_take(own, h, c, 2)
        if own:
            spread(own, x_opp, c)
            return
        d = place_of(own, x_opp)
        spread_begin(d, c)
        spread_stops(d, c, STOPS - 1, STOPS)
        ring_send(c, 0, 0)
        ring_send(c, 0, 1)
        spread_stops(d, c, 0, STOPS - 1)

    ring_copy = {}

    def ring_send(c, step, h):
        rows = pl.ds(h * HALF, HALF)
        ring_copy[c, step, h] = send(
            sp.at[c, STOPS - 1 - step, rows], rr.at[step, c, rows],
            ring_s.at[c, step, h], ring_r.at[c, step, h], previous,
        )

    def ring_step(c, step):
        s = STOPS - 2 - step
        for h in range(2):
            ring_copy[c, step, h].wait_recv()
            rows = pl.ds(h * HALF, HALF)
            if s > 0:
                sp[c, s, rows] = sp[c, s, rows] + rr[step, c, rows]
                ring_send(c, step + 1, h)
            else:
                gf[c, rows] = sp[c, 0, rows] + rr[step, c, rows]
        if s == 0:
            store(gf.at[c], gf_hbm.at[:, pl.ds(c * HALF, HALF)], 2 + c)

    ag_across(0, 0)
    red_y()
    spread(1, x, 0, first=True)
    ag_relay(1, 1, 0)
    ag_relay(1, 1, 1)
    spread(1, x, 1, first=True)
    ag_across(0, 1)
    spread_sides(1, 0)
    red_z()
    ag_relay(0, 0, 0)
    spread_sides(1, 1)
    ag_across(1, 0)
    spread(0, x, 0)
    spread_opposite(1, 0)
    ag_relay(0, 0, 1)
    spread_opposite(1, 1)
    ag_across(1, 1)
    ag_relay(0, 1, 0)
    red_x()
    spread(0, x, 1)
    spread_sides(0, 0)
    ag_relay(0, 1, 1)
    spread_opposite(0, 0)
    red_y_back()
    spread_sides(0, 1)
    ring_step(0, 0)
    spread_opposite(0, 1)
    ring_step(0, 1)
    red_core_back()
    ring_step(1, 0)
    ring_step(0, 2)
    ring_step(1, 1)
    ring_step(1, 2)
    red_copy[25].wait_recv()
    for c in range(2):
        store(gwb.at[c], gw_hbm.at[:, pl.ds(c * HALF, HALF)], 4 + c)
    for copy in stores:
        copy.wait()
    for copy in started:
        copy.wait_send()


def write_out(act, gf, gw, act_out, gf_out, gw_out, held, sems):
    loads = [
        pltpu.make_async_copy(ref, held.at[i], sems.at[i]) for i, ref in enumerate((act, gf, gw))
    ]
    stores = [
        pltpu.make_async_copy(held.at[i], ref, sems.at[3 + i])
        for i, ref in enumerate((act_out, gf_out, gw_out))
    ]
    for copy in loads:
        copy.start()
    for load, copy in zip(loads, stores):
        load.wait()
        copy.start()
    for copy in stores:
        copy.wait()


def layer(pos, count, features, weight, cotangent, tiles):
    smem = pl.BlockSpec(memory_space=pltpu.SMEM)
    hbm = pl.BlockSpec(memory_space=pltpu.HBM)
    dma = lambda *shape: pltpu.SemaphoreType.DMA(shape)
    block = (ROWS, HALF)
    piece = (HALF, HALF)
    scratch = [
        pltpu.VMEM((ROWS, HID), F32),
        pltpu.VMEM((2,) + block, F32),
        pltpu.VMEM((KMAX + 1, TILE, TILE), F32),
        pltpu.VMEM((1, TILE), jnp.int32),
        pltpu.SMEM((1, TILE), jnp.int32),
        pltpu.VMEM((HID, HID), F32),
        pltpu.VMEM((HID, HID), BF),
        pltpu.VMEM((HID, HID), BF),
        pltpu.VMEM((ROWS, HID), F32),
        pltpu.VMEM((ROWS, HID), F32),
        pltpu.VMEM((8, ROWS, 2 * BAND), BF),
        pltpu.VMEM((8, BAND, 2 * ROWS), BF),
        pltpu.VMEM((STOPS, 2) + block, F32),
        pltpu.VMEM((2, 2 * BAND, 2 * HALF), BF),
        pltpu.VMEM((4, 4, 2) + piece, F32),
        pltpu.VMEM((4, 2) + piece, F32),
        pltpu.VMEM((4, 2, 2) + piece, F32),
        pltpu.VMEM((2, 2) + piece, F32),
        pltpu.VMEM((2, 2) + piece, F32),
        pltpu.VMEM((ROWS, HID), F32),
        pltpu.VMEM((8, 2, 2) + piece, F32),
        pltpu.VMEM((2, BAND, HID), F32),
        pltpu.VMEM((2, STOPS) + block, F32),
        pltpu.VMEM((STOPS - 1, 2) + block, F32),
        pltpu.VMEM((2,) + block, F32),
        pltpu.VMEM(block, F32),
        pltpu.VMEM((NY, 32, HALF), F32),
        pltpu.VMEM((NX, 32, HALF), F32),
        pltpu.VMEM((NZ, 32, HALF), F32),
        pltpu.VMEM(block, F32),
        pltpu.VMEM((2,) + block, F32),
        dma(6), dma(6),
        dma(3, 2, 2), dma(3, 2, 2),
        dma(4, 6), dma(4, 6),
        dma(2), dma(2),
        dma(2, 2, 2, 3), dma(2, 2, 2, 3),
        dma(2, 2), dma(2, 2),
        dma(2, 3, 2), dma(2, 3, 2),
        dma(26), dma(26),
    ]
    outs = (
        jax.ShapeDtypeStruct((ROWS, HID), F32),
        jax.ShapeDtypeStruct((ROWS, HID), F32),
        jax.ShapeDtypeStruct((HID, HID), F32),
    )
    parts = pl.pallas_call(
        kernel,
        out_shape=outs,
        in_specs=[smem, smem, hbm, hbm, hbm, hbm],
        out_specs=(hbm, hbm, hbm),
        scratch_shapes=scratch,
        compiler_params=pltpu.CompilerParams(
            collective_id=0, has_side_effects=True, vmem_limit_bytes=60 << 20
        ),
        name="graph_layer",
    )(pos, count, features, weight, cotangent, tiles)
    return pl.pallas_call(
        write_out,
        out_shape=outs,
        in_specs=[hbm, hbm, hbm],
        out_specs=(hbm, hbm, hbm),
        scratch_shapes=[pltpu.VMEM((3, ROWS, HID), F32), dma(6)],
        compiler_params=pltpu.CompilerParams(vmem_limit_bytes=60 << 20),
        name="write_out",
    )(*parts)


def body(features, weight, cotangent, tile_values, tile_pos, tile_count):
    return layer(tile_pos, tile_count, features, weight, cotangent, tile_values)


def solution(mesh):
    in_specs = (
        P(("row", "rep"), None),
        P(),
        P(("row", "rep"), None),
        P("row", "rep", None, None, None),
        P("row", "rep", None),
        P("row", "rep"),
    )
    out_specs = (P(("row", "rep"), None), P(("row", "rep"), None), P())
    return jax.shard_map(body, mesh=mesh, in_specs=in_specs, out_specs=out_specs, check_vma=False)
```
